256 devices in a mesh: group: 8 (over y, core), dom: 32 (over z, x).
Axes of the slice: x: 4, y: 4, z: 8, core: 2. Of those that a mesh axis runs over, the one named last changes fastest.
Arguments:
- features: bfloat16 [131072, 256], P(('group', 'dom')), may hold values from -6 to 6
- preact: bfloat16 [131072, 256], P(('group', 'dom')), may hold values from -6 to 6
- agg_first: bfloat16 [131072, 256], P(('group', 'dom')), may hold values from -6 to 6
- agg_second: bfloat16 [131072, 256], P(('group', 'dom')), may hold values from -6 to 6
- grad_out: bfloat16 [131072, 256], P(('group', 'dom')), may hold values from -6 to 6
- self_first: bfloat16 [256, 256], replicated, may hold values from -0.375 to 0.375
- neigh_first: bfloat16 [256, 256], replicated, may hold values from -0.375 to 0.375
- self_second: bfloat16 [256, 256], replicated, may hold values from -0.375 to 0.375
- neigh_second: bfloat16 [256, 256], replicated, may hold values from -0.375 to 0.375
- tile_vals: bfloat16 [98304, 128, 128], P(('group', 'dom')), may hold values from -0.109375 to 0.109375
- tile_rows: int32 [256, 384], P(('group', 'dom')), may hold values from 0 to 15
- tile_cols: int32 [256, 384], P(('group', 'dom')), may hold values from 0 to 15
- tile_count: int32 [256], P(('group', 'dom')), may hold values from 96 to 384, as said below
- send_count: int32 [256, 32], P(('group', 'dom')), may hold values from 0 to 192, as said below
- mirror_slot: int32 [256, 32, 192], P(('group', 'dom')), may hold values from 0 to 2047, as said below
- master_row: int32 [256, 32, 192], P(('group', 'dom')), may hold values from 0 to 511
Outputs:
- input_grad: bfloat16 [131072, 256], P(('group', 'dom'))
- weight_grads: float32 [4, 256, 256], replicated
The draws below stay inside these ranges and needn't reach their ends.
Inputs may be any that keep to these rules, and one draw needn't show every extreme that they name: `send_count`: the counts of each partition sum to 2048. In every group one partition, drawn per group, has exactly 192 rows from every partition of the group, its own included. `mirror_slot`: for each partition the entries c < send_count of its 32 lists together name each of its 2048 slots exactly once; the later entries are arbitrary slots. `master_row`: entries past the sender's count are arbitrary rows. `tile_count`: tiles at or past the count are padding with arbitrary contents. Some partition uses all 384 tiles, another only 96.
All inputs are finite; a program needn't handle non-finite values.
Results may differ from the reference program's by a relative error of at most 0.0095.
Values may be sent and summed in bfloat16 or wider, within the bound.
No kernel may reach another device: no remote copies, remote signals or barrier semaphores. Data moves between devices by JAX's collectives and lax.ppermute only.
A program may use at most 128 MiB of HBM per device.

```python
import jax
import jax.numpy as jnp
from jax import lax

FEAT = 256
TILE = 128
MASTERS = 512
SLOT_BLOCKS = 16
TILES = 384
SLOTS = 2048
DOMAINS = 32
PARTITIONS = 256
CAP = 192
NODES = 131072


def group_lists(key):
    groups_n = PARTITIONS // DOMAINS
    rest = SLOTS - CAP
    base = rest // (DOMAINS - 1)
    extra = rest % (DOMAINS - 1)
    pairs = (DOMAINS - 1) // 2
    position = jnp.arange(DOMAINS, dtype=jnp.int32)

    def one_part(part_key, hot_peer):
        keys = jax.random.split(part_key, 3)
        perm = jax.random.permutation(keys[0], DOMAINS).astype(jnp.int32)
        order = jnp.where(perm == hot_peer, perm[0], perm).at[0].set(hot_peer)
        in_order = jnp.where(position == 0, CAP, base + (position - 1 < extra).astype(jnp.int32))
        shifts = jax.random.randint(keys[1], (pairs,), 0, base + 1, dtype=jnp.int32)
        pair_iota = jnp.arange(pairs, dtype=jnp.int32)
        moved = jnp.zeros((DOMAINS,), jnp.int32).at[1 + 2 * pair_iota].add(-shifts).at[2 + 2 * pair_iota].add(shifts)
        in_order = in_order + moved
        counts = jnp.zeros((DOMAINS,), jnp.int32).at[order].set(in_order)
        slot_perm = jax.random.permutation(keys[2], SLOTS).astype(jnp.int32)
        offsets = jnp.cumsum(counts) - counts
        slot_pos = (offsets[:, None] + jnp.arange(CAP, dtype=jnp.int32)[None, :]) % SLOTS
        return (counts, slot_perm[slot_pos])

    def one_group(group_key):
        keys = jax.random.split(group_key, DOMAINS + 1)
        hot_peer = jax.random.randint(keys[0], (), 0, DOMAINS, dtype=jnp.int32)
        return jax.vmap(one_part, in_axes=(0, None))(keys[1:], hot_peer)
    group_keys = jax.random.split(jax.random.fold_in(key, 11), groups_n)
    counts, slots = jax.vmap(one_group)(group_keys)
    return (counts.reshape(PARTITIONS, DOMAINS), slots.reshape(PARTITIONS, DOMAINS, CAP))


def draw_send_count(key, part):
    return group_lists(key)[0]


def draw_mirror_slot(key, part):
    return group_lists(key)[1]


def draw_tile_count(key, part):
    key = jax.random.fold_in(key, 5)
    keys = jax.random.split(key, 3)
    counts = jax.random.randint(keys[0], (PARTITIONS,), TILES // 4, TILES + 1, dtype=jnp.int32)
    full_part = jax.random.randint(keys[1], (), 0, PARTITIONS, dtype=jnp.int32)
    light_part = (full_part + 1 + jax.random.randint(keys[2], (), 0, PARTITIONS - 1, dtype=jnp.int32)) % PARTITIONS
    return counts.at[full_part].set(TILES).at[light_part].set(TILES // 4)


def with_ends(result, key, least, high):
    extent = result.shape
    spot = [jax.random.randint(jax.random.fold_in(key, axis), (), 0, extent[axis]) for axis in range(len(extent))]
    result = result.at[tuple(spot)].set(least)
    longest = extent.index(max(extent))
    spot[longest] = (spot[longest] + 1) % extent[longest]
    return result.at[tuple(spot)].set(high)


def levels(rng, shape, cuts, low, top_value):
    gain = 1.0
    for dim, parts in cuts:
        heights = jax.random.uniform(jax.random.fold_in(jax.random.fold_in(rng, 6), dim), (parts,), jnp.float32, low / len(cuts), top_value / len(cuts))
        gain = gain * jnp.repeat(jnp.exp(heights), shape[dim] // parts).reshape((-1,) + (1,) * (len(shape) - 1 - dim))
    return gain


def centred(own_key, dims, scale, bound, shards=(), held_as=jnp.bfloat16):
    factor_of = levels(own_key, dims, shards, -0.22, 0.18) if shards else 1.0
    result = jax.random.normal(own_key, dims, jnp.float32) * scale * factor_of
    return jnp.minimum(jnp.maximum(result, -bound), bound).astype(held_as)


def setup_inputs(seed: int = 0) -> dict:
    key_of = jax.random.split(jax.random.key(seed), 17)
    features = centred(key_of[0], (NODES, FEAT), 1.0, 6.0, ((0, 256),))
    preact = centred(key_of[1], (NODES, FEAT), 1.0, 6.0, ((0, 256),))
    agg_first = centred(key_of[2], (NODES, FEAT), 1.0, 6.0, ((0, 256),))
    agg_second = centred(key_of[3], (NODES, FEAT), 1.0, 6.0, ((0, 256),))
    grad_out = centred(key_of[4], (NODES, FEAT), 1.0, 6.0, ((0, 256),))
    self_first = centred(key_of[5], (FEAT, FEAT), FEAT ** -0.5, 0.375)
    neigh_first = centred(key_of[6], (FEAT, FEAT), FEAT ** -0.5, 0.375)
    self_second = centred(key_of[7], (FEAT, FEAT), FEAT ** -0.5, 0.375)
    neigh_second = centred(key_of[8], (FEAT, FEAT), FEAT ** -0.5, 0.375)
    tile_vals = centred(key_of[9], (PARTITIONS * TILES, TILE, TILE), (TILE * TILES // SLOT_BLOCKS) ** -0.5, 0.109375, ((0, 256),))
    tile_rows = with_ends(jax.random.randint(key_of[10], (PARTITIONS, TILES), 0, SLOT_BLOCKS), jax.random.fold_in(key_of[10], 1), 0, SLOT_BLOCKS - 1).astype(jnp.int32)
    tile_cols = with_ends(jax.random.randint(key_of[11], (PARTITIONS, TILES), 0, SLOT_BLOCKS), jax.random.fold_in(key_of[11], 1), 0, SLOT_BLOCKS - 1).astype(jnp.int32)
    tile_count = draw_tile_count(jax.random.fold_in(key_of[16], 71), 0)
    send_count = draw_send_count(jax.random.fold_in(key_of[16], 71), 0)
    mirror_slot = draw_mirror_slot(jax.random.fold_in(key_of[16], 71), 0)
    master_row = with_ends(jax.random.randint(key_of[15], (PARTITIONS, DOMAINS, CAP), 0, MASTERS), jax.random.fold_in(key_of[15], 1), 0, MASTERS - 1).astype(jnp.int32)
    return {"features": features, "preact": preact, "agg_first": agg_first, "agg_second": agg_second, "grad_out": grad_out, "self_first": self_first, "neigh_first": neigh_first, "self_second": self_second, "neigh_second": neigh_second, "tile_vals": tile_vals, "tile_rows": tile_rows, "tile_cols": tile_cols, "tile_count": tile_count, "send_count": send_count, "mirror_slot": mirror_slot, "master_row": master_row}


def aggregate_back(tile_block, row_ids, col_ids, tile_total, mirrored):
    blocks = mirrored.reshape(SLOT_BLOCKS, TILE, FEAT)
    picked = blocks[row_ids]
    product = jnp.einsum("tij,tif->tjf", tile_block.astype(jnp.float32), picked.astype(jnp.float32), precision=lax.Precision.HIGHEST)
    live_tiles = jnp.arange(TILES) < tile_total
    select = ((col_ids[None, :] == jnp.arange(SLOT_BLOCKS)[:, None]) & live_tiles[None, :]).astype(jnp.float32)
    summed = jnp.einsum("bt,tjf->bjf", select, product, precision=lax.Precision.HIGHEST)
    return summed.reshape(SLOTS, FEAT)


def mirror_round(pushed, tile_vals, tile_rows, tile_cols, tile_count, send_count, mirror_slot, master_row):
    tiles_all = tile_vals.reshape(PARTITIONS, TILES, TILE, TILE)
    slot_iota = jnp.arange(CAP)

    def visit_part(master_sums, part_index):
        group_first = (part_index // DOMAINS) * DOMAINS
        dom_index = part_index % DOMAINS
        owners = group_first + jnp.arange(DOMAINS)
        node_ids = owners[:, None] * MASTERS + master_row[owners, dom_index]
        live_slots = slot_iota[None, :] < send_count[part_index][:, None]
        slot_ids = jnp.where(live_slots, mirror_slot[part_index], SLOTS)
        mirrored = jnp.zeros((SLOTS, FEAT), jnp.bfloat16).at[slot_ids.reshape(-1)].set(
            pushed[node_ids].reshape(-1, FEAT), mode="drop")
        spread = aggregate_back(tiles_all[part_index], tile_rows[part_index], tile_cols[part_index],
                                tile_count[part_index], mirrored).astype(jnp.bfloat16)
        leaving = jnp.where(live_slots[:, :, None], spread[mirror_slot[part_index]].astype(jnp.float32), 0.0)
        master_sums = master_sums.at[node_ids.reshape(-1)].add(leaving.reshape(-1, FEAT))
        return master_sums, None

    scanned = lax.scan(visit_part, jnp.zeros((NODES, FEAT), jnp.float32), jnp.arange(PARTITIONS))
    return scanned[0]


def layer_back(inputs, stored, upstream, w_self, w_neigh, tile_vals, tile_rows, tile_cols, tile_count, send_count, mirror_slot, master_row):
    factor = NODES ** -0.5
    grad_self = jnp.einsum("nf,ng->fg", inputs.astype(jnp.float32), upstream.astype(jnp.float32), precision=lax.Precision.HIGHEST) * factor
    grad_neigh = jnp.einsum("nf,ng->fg", stored.astype(jnp.float32), upstream.astype(jnp.float32), precision=lax.Precision.HIGHEST) * factor
    pushed = jnp.dot(upstream, w_neigh.T, preferred_element_type=jnp.float32).astype(jnp.bfloat16)
    returned = mirror_round(pushed, tile_vals, tile_rows, tile_cols, tile_count, send_count, mirror_slot, master_row)
    layer_grad = jnp.dot(upstream, w_self.T, preferred_element_type=jnp.float32) + returned
    return layer_grad, grad_self, grad_neigh


def reference(features, preact, agg_first, agg_second, grad_out, self_first, neigh_first, self_second, neigh_second,
              tile_vals, tile_rows, tile_cols, tile_count, send_count, mirror_slot, master_row):
    activated = jnp.maximum(preact, 0.0)
    second_grad, self_two, neigh_two = layer_back(activated, agg_second, grad_out, self_second, neigh_second,
                                                  tile_vals, tile_rows, tile_cols, tile_count, send_count, mirror_slot, master_row)
    first_upstream = jnp.where(preact > 0, second_grad, 0.0).astype(jnp.bfloat16)
    first_grad, self_one, neigh_one = layer_back(features, agg_first, first_upstream, self_first, neigh_first,
                                                 tile_vals, tile_rows, tile_cols, tile_count, send_count, mirror_slot, master_row)
    return first_grad.astype(jnp.bfloat16), jnp.stack([self_one, neigh_one, self_two, neigh_two])
```

```python
import functools

import jax
import jax.numpy as jnp
from jax import lax
from jax.experimental import pallas as pl
from jax.experimental.pallas import tpu as pltpu
from jax.sharding import PartitionSpec as P

SLOTS = 2048
EDGE = 128
KSTEP = 512
BF = jnp.bfloat16
F32 = jnp.float32
BIG = 56 * 1024 * 1024


def params():
    return pltpu.CompilerParams(vmem_limit_bytes=BIG)


def dot_nt(a, b):
    return lax.dot_general(a, b, (((1,), (1,)), ((), ())), preferred_element_type=F32)


def dot_nn(a, b):
    return lax.dot_general(a, b, (((1,), (0,)), ((), ())), preferred_element_type=F32)


def wide_onehot(index_row, height):
    iota = lax.broadcasted_iota(jnp.int32, (height, index_row.shape[1]), 0).astype(F32)
    return jnp.where(iota == index_row, 1.0, 0.0).astype(BF)


def tall_onehot(index_row, width):
    column = jnp.transpose(jnp.broadcast_to(index_row, (EDGE, EDGE)))
    parts = []
    for b in range(width // EDGE):
        iota = lax.broadcasted_iota(jnp.int32, (EDGE, EDGE), 1).astype(F32) + float(b * EDGE)
        parts.append(jnp.where(column == iota, 1.0, 0.0).astype(BF))
    return jnp.concatenate(parts, axis=1)


def push_kernel(u_ref, w_ref, rows_ref, out_ref, pushed, hot):
    pushed[...] = dot_nt(u_ref[...], w_ref[...]).astype(BF)
    per = hot.shape[0] // EDGE

    def step(i, carry):
        for j in range(per):
            hot[j * EDGE : (j + 1) * EDGE, :] = tall_onehot(
                rows_ref[pl.ds(i * per + j, 1), :], hot.shape[1]
            )
        start = pl.multiple_of(i * hot.shape[0], hot.shape[0])
        out_ref[pl.ds(start, hot.shape[0]), :] = dot_nn(hot[...], pushed[...]).astype(BF)
        return carry

    lax.fori_loop(0, out_ref.shape[0] // hot.shape[0], step, 0)


def push_rows(u, w, rows):
    masters, feat = u.shape
    total = rows.size
    return pl.pallas_call(
        push_kernel,
        out_shape=jax.ShapeDtypeStruct((total, feat), BF),
        scratch_shapes=[pltpu.VMEM((masters, feat), BF), pltpu.VMEM((1024, masters), BF)],
        compiler_params=params(),
        cost_estimate=pl.CostEstimate(
            flops=2 * total * masters * feat, bytes_accessed=total * feat * 2, transcendentals=0
        ),
        name="push_rows",
    )(u, w, rows.reshape(-1, EDGE))


def dense_kernel(rows_ref, cols_ref, count_ref, vals_ref, out_ref, acc):
    step = pl.program_id(0)
    per = vals_ref.shape[0]

    @pl.when(step == 0)
    def _():
        def clear(i, carry):
            acc[i] = jnp.zeros((EDGE, EDGE), F32)
            return carry

        lax.fori_loop(0, acc.shape[0], clear, 0)

    first = step * per
    live = jnp.clip(count_ref[0] - first, 0, per)

    def add(i, carry):
        at = rows_ref[first + i] * 16 + cols_ref[first + i]
        acc[at] += vals_ref[i].astype(F32)
        return carry

    lax.fori_loop(0, live, add, 0)

    @pl.when(step == pl.num_programs(0) - 1)
    def _():
        def flip(j, carry):
            start = pl.multiple_of(j * EDGE, EDGE)
            for i in range(16):
                block = jnp.transpose(acc[i * 16 + j]).astype(BF)
                lane = (i % 4) * EDGE
                out_ref[i // 4, pl.ds(start, EDGE), lane : lane + EDGE] = block
            return carry

        lax.fori_loop(0, 16, flip, 0)


def dense_adjacency(tile_vals, rows, cols, count):
    tiles = tile_vals.shape[0]
    per = 32
    return pl.pallas_call(
        dense_kernel,
        out_shape=jax.ShapeDtypeStruct((SLOTS // KSTEP, SLOTS, KSTEP), BF),
        grid_spec=pltpu.PrefetchScalarGridSpec(
            num_scalar_prefetch=3,
            grid=(tiles // per,),
            in_specs=[pl.BlockSpec((per, EDGE, EDGE), lambda i, *_: (i, 0, 0))],
            out_specs=pl.BlockSpec((SLOTS // KSTEP, SLOTS, KSTEP), lambda i, *_: (0, 0, 0)),
            scratch_shapes=[pltpu.VMEM((256, EDGE, EDGE), F32)],
        ),
        compiler_params=params(),
        cost_estimate=pl.CostEstimate(
            flops=tiles * EDGE * EDGE * 64, bytes_accessed=40 * 2**20, transcendentals=0
        ),
        name="dense_adjacency",
    )(rows, cols, count, tile_vals)


def spread_kernel(arrived_ref, slots_ref, slots_wide_ref, adj_hbm, out_ref, adj, acc, rows, sem):
    load = pltpu.make_async_copy(adj_hbm, adj, sem)
    load.start()
    acc[...] = jnp.zeros_like(acc)

    def place(k, carry):
        hot = wide_onehot(slots_wide_ref[pl.ds(k, 1), :], SLOTS)
        start = pl.multiple_of(k * KSTEP, KSTEP)
        acc[...] += dot_nn(hot, arrived_ref[pl.ds(start, KSTEP), :])
        return carry

    lax.fori_loop(0, arrived_ref.shape[0] // KSTEP, place, 0)
    rows[...] = acc[...].astype(BF)
    acc[...] = jnp.zeros_like(acc)
    load.wait()

    def multiply(k, carry):
        start = pl.multiple_of(k * KSTEP, KSTEP)
        acc[...] += dot_nn(adj[k], rows[pl.ds(start, KSTEP), :])
        return carry

    lax.fori_loop(0, SLOTS // KSTEP, multiply, 0)
    rows[...] = acc[...].astype(BF)
    per = 1024 // EDGE

    def collect(k, carry):
        hot = jnp.concatenate(
            [tall_onehot(slots_ref[pl.ds(k * per + j, 1), :], SLOTS) for j in range(per)], axis=0
        )
        start = pl.multiple_of(k * 1024, 1024)
        out_ref[pl.ds(start, 1024), :] = dot_nn(hot, rows[...]).astype(BF)
        return carry

    lax.fori_loop(0, out_ref.shape[0] // 1024, collect, 0)


def spread_rows(arrived, slots, adj):
    total, feat = arrived.shape
    vmem = pl.BlockSpec(memory_space=pltpu.VMEM)
    return pl.pallas_call(
        spread_kernel,
        out_shape=jax.ShapeDtypeStruct((total, feat), BF),
        in_specs=[vmem, vmem, vmem, pl.BlockSpec(memory_space=pl.ANY)],
        out_specs=vmem,
        scratch_shapes=[
            pltpu.VMEM(adj.shape, BF),
            pltpu.VMEM((SLOTS, feat), F32),
            pltpu.VMEM((SLOTS, feat), BF),
            pltpu.SemaphoreType.DMA,
        ],
        compiler_params=params(),
        cost_estimate=pl.CostEstimate(
            flops=4 * total * SLOTS * feat, bytes_accessed=14 * 2**20, transcendentals=0
        ),
        name="spread_rows",
    )(arrived, slots.reshape(-1, EDGE), slots.reshape(-1, KSTEP), adj)


def gather_kernel(masked, landed_ref, rows_ref, u_ref, w_ref, *rest):
    if masked:
        pre_ref, out_ref, acc = rest
    else:
        out_ref, acc = rest
    acc[...] = dot_nt(u_ref[...], w_ref[...])

    def step(k, carry):
        hot = wide_onehot(rows_ref[pl.ds(k, 1), :], acc.shape[0])
        start = pl.multiple_of(k * KSTEP, KSTEP)
        acc[...] += dot_nn(hot, landed_ref[pl.ds(start, KSTEP), :])
        return carry

    lax.fori_loop(0, landed_ref.shape[0] // KSTEP, step, 0)
    if masked:
        out_ref[...] = jnp.where(pre_ref[...].astype(F32) > 0.0, acc[...], 0.0).astype(BF)
    else:
        out_ref[...] = acc[...].astype(BF)


def gather_back(landed, rows, u, w, preact):
    args = [landed, rows.reshape(-1, KSTEP), u, w] + ([] if preact is None else [preact])
    total, feat = landed.shape
    return pl.pallas_call(
        functools.partial(gather_kernel, preact is not None),
        out_shape=jax.ShapeDtypeStruct(u.shape, BF),
        scratch_shapes=[pltpu.VMEM(u.shape, F32)],
        compiler_params=params(),
        cost_estimate=pl.CostEstimate(
            flops=2 * total * u.shape[0] * feat, bytes_accessed=total * feat * 2, transcendentals=0
        ),
        name="gather_back",
    )(*args)


def on_device(
    features,
    preact,
    agg_first,
    agg_second,
    grad_out,
    self_first,
    neigh_first,
    self_second,
    neigh_second,
    tile_vals,
    tile_rows,
    tile_cols,
    tile_count,
    send_count,
    mirror_slot,
    master_row,
):
    domains = lax.axis_size("dom")
    groups = lax.axis_size("group")
    masters, feat = features.shape
    factor = (masters * domains * groups) ** (-0.5)
    capacity = mirror_slot.shape[2]
    rows = master_row[0].astype(F32)
    live = jnp.arange(capacity)[None, :] < send_count[0][:, None]
    slots = jnp.where(live, mirror_slot[0], -1).astype(F32)

    def swap(x, axis="dom"):
        return lax.all_to_all(x, axis, split_axis=0, concat_axis=0, tiled=True)

    def swap_rows(x):
        return swap(x.reshape(domains, capacity, feat)).reshape(-1, feat)

    def grads(inputs, stored, upstream):
        both = [
            jnp.einsum("nf,ng->fg", part, upstream, preferred_element_type=F32)
            for part in (inputs, stored)
        ]
        return jnp.concatenate(both, axis=0) * factor

    def sum_everywhere(total):
        height = total.shape[0] // groups
        part = jnp.sum(swap(total.reshape(groups, height, feat), "group"), axis=0)
        piece = jnp.sum(swap(part.reshape(domains, height // domains, feat)), axis=0)
        part = swap(jnp.broadcast_to(piece, (domains,) + piece.shape)).reshape(height, feat)
        return swap(jnp.broadcast_to(part, (groups,) + part.shape), "group").reshape(-1, feat)

    activated = jnp.maximum(preact, 0.0)
    arrived = swap_rows(push_rows(grad_out, neigh_second, rows))
    adj = dense_adjacency(tile_vals, tile_rows[0], tile_cols[0], tile_count)
    weights_two = lax.psum(grads(activated, agg_second, grad_out), ("group", "dom"))
    landed = swap_rows(spread_rows(arrived, slots, adj))
    upstream = gather_back(landed, rows, grad_out, self_second, preact)

    arrived = swap_rows(push_rows(upstream, neigh_first, rows))
    weights_one = sum_everywhere(grads(features, agg_first, upstream))
    landed = swap_rows(spread_rows(arrived, slots, adj))
    input_grad = gather_back(landed, rows, upstream, self_first, None)
    weight_grads = jnp.concatenate([weights_one, weights_two], axis=0).reshape(4, feat, feat)
    return (input_grad, weight_grads)


def solution(mesh):
    every = ("group", "dom")
    in_specs = (
        (P(every, None),) * 5
        + (P(),) * 4
        + (P(every, None, None), P(every, None), P(every, None), P(every), P(every, None))
        + (P(every, None, None),) * 2
    )
    out_specs = (P(every, None), P())
    return jax.shard_map(
        on_device, mesh=mesh, in_specs=in_specs, out_specs=out_specs, check_vma=False
    )
```

```python
import functools

import jax
import jax.numpy as jnp
from jax import lax
from jax.experimental import pallas as pl
from jax.experimental.pallas import tpu as pltpu
from jax.sharding import PartitionSpec as P

SLOTS = 2048
EDGE = 128
KSTEP = 512
BF = jnp.bfloat16
F32 = jnp.float32
BIG = 56 * 1024 * 1024


def params():
    return pltpu.CompilerParams(vmem_limit_bytes=BIG)


def dot_nt(a, b):
    return lax.dot_general(a, b, (((1,), (1,)), ((), ())), preferred_element_type=F32)


def dot_nn(a, b):
    return lax.dot_general(a, b, (((1,), (0,)), ((), ())), preferred_element_type=F32)


def wide_onehot(index_row, height):
    iota = lax.broadcasted_iota(jnp.int32, (height, index_row.shape[1]), 0).astype(F32)
    return jnp.where(iota == index_row, 1.0, 0.0).astype(BF)


def tall_onehot(index_row, width):
    column = jnp.transpose(jnp.broadcast_to(index_row, (EDGE, EDGE)))
    parts = []
    for b in range(width // EDGE):
        iota = lax.broadcasted_iota(jnp.int32, (EDGE, EDGE), 1).astype(F32) + float(b * EDGE)
        parts.append(jnp.where(column == iota, 1.0, 0.0).astype(BF))
    return jnp.concatenate(parts, axis=1)


def dense_kernel(rows_ref, cols_ref, count_ref, vals_ref, out_ref, acc):
    step = pl.program_id(0)
    per = vals_ref.shape[0]

    @pl.when(step == 0)
    def _():
        def clear(i, carry):
            acc[i] = jnp.zeros((EDGE, EDGE), F32)
            return carry

        lax.fori_loop(0, acc.shape[0], clear, 0)

    first = step * per
    live = jnp.clip(count_ref[0] - first, 0, per)

    def add(i, carry):
        at = rows_ref[first + i] * 16 + cols_ref[first + i]
        acc[at] += vals_ref[i].astype(F32)
        return carry

    lax.fori_loop(0, live, add, 0)

    @pl.when(step == pl.num_programs(0) - 1)
    def _():
        def flip(j, carry):
            start = pl.multiple_of(j * EDGE, EDGE)
            for i in range(16):
                block = jnp.transpose(acc[i * 16 + j]).astype(BF)
                lane = (i % 4) * EDGE
                out_ref[i // 4, pl.ds(start, EDGE), lane : lane + EDGE] = block
            return carry

        lax.fori_loop(0, 16, flip, 0)


def dense_adjacency(tile_vals, rows, cols, count):
    tiles = tile_vals.shape[0]
    per = 32
    return pl.pallas_call(
        dense_kernel,
        out_shape=jax.ShapeDtypeStruct((SLOTS // KSTEP, SLOTS, KSTEP), BF),
        grid_spec=pltpu.PrefetchScalarGridSpec(
            num_scalar_prefetch=3,
            grid=(tiles // per,),
            in_specs=[pl.BlockSpec((per, EDGE, EDGE), lambda i, *_: (i, 0, 0))],
            out_specs=pl.BlockSpec((SLOTS // KSTEP, SLOTS, KSTEP), lambda i, *_: (0, 0, 0)),
            scratch_shapes=[pltpu.VMEM((256, EDGE, EDGE), F32)],
        ),
        compiler_params=params(),
        cost_estimate=pl.CostEstimate(
            flops=tiles * EDGE * EDGE * 64, bytes_accessed=40 * 2**20, transcendentals=0
        ),
        name="dense_adjacency",
    )(rows, cols, count, tile_vals)


def cost(flops, size):
    return pl.CostEstimate(flops=flops, bytes_accessed=size, transcendentals=0)


def tall_rows(index_ref, first, count, width):
    return jnp.concatenate(
        [tall_onehot(index_ref[first + j : first + j + 1, :], width) for j in range(count)], axis=0
    )


def split_rows(value, outs):
    size = outs[0].shape[0]
    for j, out in enumerate(outs):
        out[...] = value[j * size : (j + 1) * size, :]


def pick_kernel(parts, index_ref, *refs):
    sources, outs = refs[: sum(parts)], refs[sum(parts) :]
    cap = outs[0].shape[0] // len(parts)
    per = 4 * cap // EDGE
    at = 0
    for b, pieces in enumerate(parts):
        block = jnp.concatenate([r[...] for r in sources[at : at + pieces]], axis=0)
        at += pieces
        hot = tall_rows(index_ref, b * per, per, block.shape[0])
        rows = dot_nn(hot, block).astype(BF)
        for j in range(4):
            outs[j][b * cap : (b + 1) * cap, :] = rows[j * cap : (j + 1) * cap, :]


def pick_rows(blocks, index):
    feat = blocks[0][0].shape[1]
    n, _, cap = index.shape
    return pl.pallas_call(
        functools.partial(pick_kernel, tuple(len(b) for b in blocks)),
        out_shape=[jax.ShapeDtypeStruct((n * cap, feat), BF)] * 4,
        compiler_params=params(),
        cost_estimate=cost(8 * n * cap * 512 * feat, n * 2**20),
        name="pick_rows",
    )(index.reshape(-1, EDGE), *[piece for b in blocks for piece in b])


def add_slots(acc, slots_ref, piece, arrays):
    hot = wide_onehot(slots_ref[piece : piece + 1, :], SLOTS)
    acc[...] += dot_nn(hot, jnp.concatenate([a[...] for a in arrays], axis=0))


def add_chunks(acc, slots_ref, refs, sizes):
    piece = 0
    for c, n in enumerate(sizes):
        arrays = refs[4 * c : 4 * c + 4]
        step = 4 // n
        for j in range(n):
            add_slots(acc, slots_ref, piece, arrays[j * step : (j + 1) * step])
            piece += 1


def early_kernel(sizes, slots_ref, *refs):
    out = refs[-1]
    out[...] = jnp.zeros_like(out)
    add_chunks(out, slots_ref, refs[:-1], sizes)


def early_slots(chunks, slots, sizes):
    feat = chunks[0][0].shape[1]
    return pl.pallas_call(
        functools.partial(early_kernel, sizes),
        out_shape=jax.ShapeDtypeStruct((SLOTS, feat), F32),
        compiler_params=params(),
        cost_estimate=cost(2 * SLOTS * 768 * feat * sum(sizes), 8 * 2**20),
        name="early_slots",
    )(slots, *[a for c in chunks for a in c])


def leave(index_ref, spread, outs):
    hot = tall_rows(index_ref, 0, index_ref.shape[0], SLOTS)
    split_rows(dot_nn(hot, spread).astype(BF), outs)


def spread_kernel(sizes, slots_ref, index_ref, acc_in, adj_hbm, *refs):
    count = 4 * len(sizes)
    arrays, spread, outs = refs[:count], refs[count], refs[count + 1 : count + 5]
    adj, acc, sem = refs[count + 5 :]
    load = pltpu.make_async_copy(adj_hbm, adj, sem)
    load.start()
    acc[...] = acc_in[...]
    add_chunks(acc, slots_ref, arrays, sizes)
    spread[...] = acc[...].astype(BF)
    acc[...] = jnp.zeros_like(acc)
    load.wait()

    def multiply(k, carry):
        start = pl.multiple_of(k * KSTEP, KSTEP)
        acc[...] += dot_nn(adj[k], spread[pl.ds(start, KSTEP), :])
        return carry

    lax.fori_loop(0, SLOTS // KSTEP, multiply, 0)
    spread[...] = acc[...].astype(BF)
    leave(index_ref, spread[...], outs)


def spread_rows(acc, chunks, slots, sizes, adj, index):
    feat = acc.shape[1]
    cap = index.shape[1] * index.shape[2]
    vmem = pl.BlockSpec(memory_space=pltpu.VMEM)
    arrays = [a for c in chunks for a in c]
    return pl.pallas_call(
        functools.partial(spread_kernel, sizes),
        out_shape=[jax.ShapeDtypeStruct((SLOTS, feat), BF)]
        + [jax.ShapeDtypeStruct((cap, feat), BF)] * 4,
        in_specs=[vmem, vmem, vmem, pl.BlockSpec(memory_space=pl.ANY)] + [vmem] * len(arrays),
        scratch_shapes=[
            pltpu.VMEM(adj.shape, BF),
            pltpu.VMEM((SLOTS, feat), F32),
            pltpu.SemaphoreType.DMA,
        ],
        compiler_params=params(),
        cost_estimate=cost(2 * SLOTS * feat * (SLOTS + 768 * (sum(sizes) + 1)), 16 * 2**20),
        name="spread_rows",
    )(slots, index.reshape(-1, EDGE), acc, adj, *arrays)


def leave_kernel(index_ref, spread_ref, *outs):
    leave(index_ref, spread_ref[...], outs)


def leave_rows(spread, index):
    feat = spread.shape[1]
    cap = index.shape[1] * index.shape[2]
    return pl.pallas_call(
        leave_kernel,
        out_shape=[jax.ShapeDtypeStruct((cap, feat), BF)] * 4,
        compiler_params=params(),
        cost_estimate=cost(8 * cap * SLOTS * feat, 3 * 2**20),
        name="leave_rows",
    )(index.reshape(-1, EDGE), spread)


def partial_sum(rows_ref, landed, block, masters):
    cap = rows_ref.shape[1] // 4
    rows = jnp.concatenate([a[block * cap : (block + 1) * cap, :] for a in landed], axis=0)
    return dot_nn(wide_onehot(rows_ref[block : block + 1, :], masters), rows)


def far_kernel(rows_ref, *refs):
    total = partial_sum(rows_ref, refs[:4], 0, 512).astype(BF)
    split_rows(total, refs[4:])


def far_sums(landed, rows):
    feat = landed[0].shape[1]
    return pl.pallas_call(
        far_kernel,
        out_shape=[jax.ShapeDtypeStruct((256, feat), BF)] * 2,
        compiler_params=params(),
        cost_estimate=cost(2 * 512 * 768 * feat, 2**20),
        name="far_sums",
    )(rows, *landed)


def ring_kernel(halves, rows_ref, down_ref, up_ref, *refs):
    landed, (down_out, up_out) = refs[:4], refs[4:]
    down = partial_sum(rows_ref, landed, 0, 512)
    up = partial_sum(rows_ref, landed, 1, 512)
    if halves:
        down_out[0:256, :] = down[0:256].astype(BF)
        down_out[256:512, :] = (down[256:512] + down_ref[...].astype(F32)).astype(BF)
        up_out[0:256, :] = (up[0:256] + up_ref[...].astype(F32)).astype(BF)
        up_out[256:512, :] = up[256:512].astype(BF)
    else:
        down_out[...] = (down + down_ref[...].astype(F32)).astype(BF)
        up_out[...] = (up + up_ref[...].astype(F32)).astype(BF)


def ring_sums(landed, rows, down, up):
    feat = landed[0].shape[1]
    return pl.pallas_call(
        functools.partial(ring_kernel, down.shape[0] == 256),
        out_shape=[jax.ShapeDtypeStruct((512, feat), BF)] * 2,
        compiler_params=params(),
        cost_estimate=cost(4 * 512 * 768 * feat, 2 * 2**20),
        name="ring_sums",
    )(rows, down, up, *landed)


def own_kernel(masked, rows_ref, own_ref, down_ref, up_ref, *refs):
    landed, out = refs[:4], refs[-1]
    total = own_ref[...] + partial_sum(rows_ref, landed, 0, 512)
    total = total + down_ref[...].astype(F32) + up_ref[...].astype(F32)
    if masked:
        total = jnp.where(refs[4][...].astype(F32) > 0.0, total, 0.0)
    out[...] = total.astype(BF)


def own_sums(landed, rows, own, down, up, preact):
    args = [rows, own, down, up, *landed] + ([] if preact is None else [preact])
    feat = landed[0].shape[1]
    return pl.pallas_call(
        functools.partial(own_kernel, preact is not None),
        out_shape=jax.ShapeDtypeStruct(own.shape, BF),
        compiler_params=params(),
        cost_estimate=cost(2 * 512 * 768 * feat, 2 * 2**20),
        name="own_sums",
    )(*args)


def on_device(
    features,
    preact,
    agg_first,
    agg_second,
    grad_out,
    self_first,
    neigh_first,
    self_second,
    neigh_second,
    tile_vals,
    tile_rows,
    tile_cols,
    tile_count,
    send_count,
    mirror_slot,
    master_row,
):
    groups = lax.axis_size("group")
    domains = lax.axis_size("dom")
    masters, feat = features.shape
    factor = (masters * domains * groups) ** (-0.5)
    cap = mirror_slot.shape[2]
    nx, nz = 4, domains // 4
    here = lax.axis_index("dom")
    my_z, my_x = here // nx, here % nx
    chunks = ((0,), (-1, 1), (-2, 2), (-3, 3), (4,))
    sizes = tuple(len(c) for c in chunks)

    def z_step(x, by):
        pairs = [(z * nx + c, (z + by) % nz * nx + c) for z in range(nz) for c in range(nx)]
        return lax.ppermute(x, "dom", pairs)

    def x_step(x, by):
        pairs = [(z * nx + c, z * nx + (c + by) % nx) for z in range(nz) for c in range(nx)]
        return lax.ppermute(x, "dom", pairs)

    def x_swap(parts):
        return [parts[0]] + [x_step(parts[j], j) for j in (1, 2, 3)]

    def turn(x, by, axis):
        return lax.dynamic_slice_in_dim(jnp.concatenate([x, x], axis), by, x.shape[axis], axis)

    own_lists = master_row[0].reshape(nz, nx * cap)
    z_groups = [[z * nx + c for z in range(nz)] for c in range(nx)]
    all_lists = lax.all_to_all(own_lists, "dom", 0, 0, axis_index_groups=z_groups, tiled=True)
    near = lax.dynamic_slice_in_dim(own_lists, my_z, 1, 0).reshape(1, nx, cap)
    near = turn(near, my_x, 1).astype(F32)
    rows = turn(turn(all_lists.reshape(nz, nx, cap), my_z, 0), my_x, 1).astype(F32)
    live = jnp.arange(cap)[None, :] < send_count[0][:, None]
    slots = jnp.where(live, mirror_slot[0], -1).reshape(nz, nx, cap)
    slots = turn(turn(slots, my_z, 0), my_x, 1).astype(F32)

    def chunk_of(lists, c):
        return jnp.stack([lists[k % nz] for k in chunks[c]])

    def back(lists):
        return jnp.stack([lists[:, -j % nx] for j in range(nx)], axis=1)

    pick_lists = [near] + [chunk_of(rows, c) for c in range(1, 5)]
    sum_lists = [chunk_of(back(rows), c).reshape(-1, nx * cap) for c in range(5)]
    put_lists = [
        chunk_of(back(slots), c).transpose(1, 0, 2).reshape(-1, nx * cap) for c in range(5)
    ]
    leave_lists = [chunk_of(slots, c).transpose(1, 0, 2) for c in range(5)]
    put_early = jnp.concatenate(put_lists[:3], axis=0)
    put_late = jnp.concatenate(put_lists[3:], axis=0)

    def mirror_push(pushed):
        half = masters // 2
        down, up = [pushed], [pushed]
        arrived = [x_swap(pick_rows([(pushed,)], pick_lists[0]))]
        for c in (1, 2, 3):
            down.append(z_step(down[-1], 1))
            up.append(z_step(up[-1], -1))
            arrived.append(x_swap(pick_rows([(down[c],), (up[c],)], pick_lists[c])))
        far = (z_step(down[3][:half], 1), z_step(up[3][half:], -1))
        arrived.append(x_swap(pick_rows([far], pick_lists[4])))
        return arrived

    def mirror_return(arrived, adj):
        acc = early_slots(arrived[:3], put_early, sizes[:3])
        spread, *parts = spread_rows(acc, arrived[3:], put_late, sizes[3:], adj, leave_lists[4])
        landed = {4: x_swap(parts)}
        for c in (3, 2, 1, 0):
            landed[c] = x_swap(leave_rows(spread, leave_lists[c]))
        up, down = far_sums(landed[4], sum_lists[4])
        up, down = z_step(up, 1), z_step(down, -1)
        for c in (3, 2, 1):
            down, up = ring_sums(landed[c], sum_lists[c], down, up)
            up, down = z_step(up, 1), z_step(down, -1)
        return landed[0], down, up

    def layer_back(upstream, w_self, w_neigh, adj, mask):
        pushed = jnp.einsum("nf,gf->ng", upstream, w_neigh, preferred_element_type=F32).astype(BF)
        arrived = mirror_push(pushed)
        own = jnp.einsum("nf,gf->ng", upstream, w_self, preferred_element_type=F32)
        landed, down, up = mirror_return(arrived, adj)
        return own_sums(landed, sum_lists[0], own, down, up, mask)

    def swap(x, axis="dom"):
        return lax.all_to_all(x, axis, split_axis=0, concat_axis=0, tiled=True)

    def grads(inputs, stored, upstream):
        both = [
            jnp.einsum("nf,ng->fg", part, upstream, preferred_element_type=F32)
            for part in (inputs, stored)
        ]
        return jnp.concatenate(both, axis=0) * factor

    def scatter_sum(total):
        height = total.shape[0] // groups
        part = jnp.sum(swap(total.reshape(groups, height, feat), "group"), axis=0)
        return jnp.sum(swap(part.reshape(domains, height // domains, feat)), axis=0)

    def gather_axis(part, axis):
        size = lax.axis_size(axis)
        here = lax.axis_index(axis)
        step = 1
        while step < size:
            pairs = [(i, i ^ step) for i in range(size)]
            other = lax.ppermute(part, axis, pairs)
            upper = (here // step) % 2 == 1
            part = jnp.concatenate(
                [jnp.where(upper, other, part), jnp.where(upper, part, other)], axis=0
            )
            step *= 2
        return part

    activated = jnp.maximum(preact, 0.0)
    adj = dense_adjacency(tile_vals, tile_rows[0], tile_cols[0], tile_count)
    weights_two = grads(activated, agg_second, grad_out)
    upstream = layer_back(grad_out, self_second, neigh_second, adj, preact)
    weights_one = grads(features, agg_first, upstream)
    piece = scatter_sum(jnp.concatenate([weights_one, weights_two], axis=0))
    input_grad = layer_back(upstream, self_first, neigh_first, adj, None)
    weights = gather_axis(gather_axis(piece, "dom"), "group")
    return (input_grad, weights.reshape(4, feat, feat))


def solution(mesh):
    every = ("group", "dom")
    in_specs = (
        (P(every, None),) * 5
        + (P(),) * 4
        + (P(every, None, None), P(every, None), P(every, None), P(every), P(every, None))
        + (P(every, None, None),) * 2
    )
    out_specs = (P(every, None), P())
    return jax.shard_map(
        on_device, mesh=mesh, in_specs=in_specs, out_specs=out_specs, check_vma=False
    )
```

```python
import functools

import jax
import jax.numpy as jnp
from jax import lax
from jax.experimental import pallas as pl
from jax.experimental.pallas import tpu as pltpu
from jax.sharding import PartitionSpec as P

SLOTS = 2048
EDGE = 128
KSTEP = 512
BF = jnp.bfloat16
F32 = jnp.float32
BIG = 56 * 1024 * 1024


def params():
    return pltpu.CompilerParams(vmem_limit_bytes=BIG)


def dot_nt(a, b):
    return lax.dot_general(a, b, (((1,), (1,)), ((), ())), preferred_element_type=F32)


def dot_nn(a, b):
    return lax.dot_general(a, b, (((1,), (0,)), ((), ())), preferred_element_type=F32)


def wide_onehot(index_row, height):
    high = jnp.floor(index_row * (1.0 / EDGE))
    low = index_row - high * EDGE
    iota = lax.broadcasted_iota(jnp.int32, (EDGE, index_row.shape[1]), 0).astype(F32)
    base = jnp.where(iota == low, 1.0, 0.0).astype(BF)
    parts = [
        base * jnp.where(high == float(b), 1.0, 0.0).astype(BF) for b in range(height // EDGE)
    ]
    return jnp.concatenate(parts, axis=0)


def tall_onehot(index_row, width):
    column = jnp.transpose(jnp.broadcast_to(index_row, (EDGE, EDGE)))
    high = jnp.floor(column * (1.0 / EDGE))
    low = column - high * EDGE
    iota = lax.broadcasted_iota(jnp.int32, (EDGE, EDGE), 1).astype(F32)
    base = jnp.where(iota == low, 1.0, 0.0).astype(BF)
    high = high.astype(BF)
    none = jnp.zeros_like(base)
    parts = [jnp.where(high == jnp.full_like(high, b), base, none) for b in range(width // EDGE)]
    return jnp.concatenate(parts, axis=1)


def dense_kernel(rows_ref, cols_ref, count_ref, vals_ref, after_ref, out_ref, acc):
    step = pl.program_id(0)
    per = vals_ref.shape[0]

    @pl.when(step == 0)
    def _():
        def clear(i, carry):
            acc[i] = jnp.zeros((EDGE, EDGE), F32)
            return carry

        lax.fori_loop(0, acc.shape[0], clear, 0)

    first = step * per
    live = jnp.clip(count_ref[0] - first, 0, per)

    def add(i, carry):
        at = rows_ref[first + i] * 16 + cols_ref[first + i]
        acc[at] += vals_ref[i].astype(F32)
        return carry

    lax.fori_loop(0, live, add, 0)

    @pl.when(step == pl.num_programs(0) - 1)
    def _():
        def flip(j, carry):
            start = pl.multiple_of(j * EDGE, EDGE)
            for i in range(16):
                block = jnp.transpose(acc[i * 16 + j]).astype(BF)
                lane = (i % 4) * EDGE
                out_ref[i // 4, pl.ds(start, EDGE), lane : lane + EDGE] = block
            return carry

        lax.fori_loop(0, 16, flip, 0)


def dense_adjacency(tile_vals, rows, cols, count, after):
    tiles = tile_vals.shape[0]
    per = 32
    return pl.pallas_call(
        dense_kernel,
        out_shape=jax.ShapeDtypeStruct((SLOTS // KSTEP, SLOTS, KSTEP), BF),
        grid_spec=pltpu.PrefetchScalarGridSpec(
            num_scalar_prefetch=3,
            grid=(tiles // per,),
            in_specs=[
                pl.BlockSpec((per, EDGE, EDGE), lambda i, *_: (i, 0, 0)),
                pl.BlockSpec(memory_space=pl.ANY),
            ],
            out_specs=pl.BlockSpec((SLOTS // KSTEP, SLOTS, KSTEP), lambda i, *_: (0, 0, 0)),
            scratch_shapes=[pltpu.VMEM((256, EDGE, EDGE), F32)],
        ),
        compiler_params=params(),
        cost_estimate=cost(1, 1),
        name="dense_adjacency",
    )(rows, cols, count, tile_vals, after)


def cost(flops, size):
    return pl.CostEstimate(flops=flops, bytes_accessed=size, transcendentals=0)


def tall_rows(index_ref, first, count, width):
    return jnp.concatenate(
        [tall_onehot(index_ref[first + j : first + j + 1, :], width) for j in range(count)], axis=0
    )


def split_rows(value, outs):
    size = outs[0].shape[0]
    for j, out in enumerate(outs):
        out[...] = value[j * size : (j + 1) * size, :]


def tie_kernel(*refs):
    pass


def tie(arrays, after):
    anywhere = pl.BlockSpec(memory_space=pl.ANY)
    return pl.pallas_call(
        tie_kernel,
        out_shape=[jax.ShapeDtypeStruct(a.shape, a.dtype) for a in arrays],
        in_specs=[anywhere] * (len(arrays) + 1),
        out_specs=[anywhere] * len(arrays),
        input_output_aliases={i: i for i in range(len(arrays))},
        cost_estimate=cost(1, 1),
        name="tie",
    )(*arrays, after)


def pick_kernel(first, parts, waits, index_ref, *refs):
    refs = refs[waits:]
    sources, outs = refs[: sum(parts)], refs[sum(parts) :]
    cap = outs[0].shape[0] // len(parts)
    per = 4 * cap // EDGE
    at = 0
    for b, pieces in enumerate(parts):
        block = jnp.concatenate([r[...] for r in sources[at : at + pieces]], axis=0)
        at += pieces
        hot = tall_rows(index_ref, (first + b) * per, per, block.shape[0])
        rows = dot_nn(hot, block).astype(BF)
        for j in range(4):
            outs[j][b * cap : (b + 1) * cap, :] = rows[j * cap : (j + 1) * cap, :]


def pick_rows(blocks, index, first, after):
    feat = blocks[0][0].shape[1]
    n = len(blocks)
    cap = index.size // 32
    vmem = pl.BlockSpec(memory_space=pltpu.VMEM)
    return pl.pallas_call(
        functools.partial(pick_kernel, first, tuple(len(b) for b in blocks), len(after)),
        out_shape=[jax.ShapeDtypeStruct((n * cap, feat), BF)] * 4,
        in_specs=[vmem]
        + [pl.BlockSpec(memory_space=pl.ANY)] * len(after)
        + [vmem] * sum(len(b) for b in blocks),
        compiler_params=params(),
        cost_estimate=cost(8 * n * cap * 512 * feat, n * 2**20),
        name="pick_rows",
    )(index, *after, *[piece for b in blocks for piece in b])


def add_chunk(acc, stage, slots_ref, first, arrays):
    size = arrays[0].shape[0]
    for j, a in enumerate(arrays):
        stage[j * size : (j + 1) * size, :] = a[...]
    width = slots_ref.shape[1]
    for p in range(4 * size // width):
        hot = wide_onehot(slots_ref[first + p : first + p + 1, :], SLOTS)
        acc[...] += dot_nn(hot, stage[p * width : (p + 1) * width, :])


def early_kernel(first, slots_ref, after_ref, *refs):
    out, stage = refs[-2:]
    if len(refs) == 7:
        out[...] = refs[4][...]
    else:
        out[...] = jnp.zeros_like(out)
    add_chunk(out, stage, slots_ref, first, refs[:4])


def early_slots(arrays, acc, slots, first, after):
    size, feat = arrays[0].shape
    vmem = pl.BlockSpec(memory_space=pltpu.VMEM)
    args = [*arrays] + ([] if acc is None else [acc])
    return pl.pallas_call(
        functools.partial(early_kernel, first),
        out_shape=jax.ShapeDtypeStruct((SLOTS, feat), F32),
        in_specs=[vmem, pl.BlockSpec(memory_space=pl.ANY)] + [vmem] * len(args),
        scratch_shapes=[pltpu.VMEM((4 * size, feat), BF)],
        compiler_params=params(),
        cost_estimate=cost(1, 1),
        name="early_slots",
    )(slots, after, *args)


def leave(index_ref, first, spread_ref, outs):
    size = outs[0].shape[0]
    per = 2 * size // EDGE
    for h in range(2):
        hot = tall_rows(index_ref, first + h * per, per, SLOTS)
        rows = dot_nn(hot, spread_ref[...]).astype(BF)
        outs[2 * h][...] = rows[:size, :]
        outs[2 * h + 1][...] = rows[size:, :]


def spread_kernel(slot_first, leave_first, slots_ref, index_ref, acc_in, adj_hbm, *refs):
    arrays, spread, outs = refs[:4], refs[4], refs[5:9]
    adj, acc, stage, sem = refs[9:]
    load = pltpu.make_async_copy(adj_hbm, adj, sem)
    load.start()
    acc[...] = acc_in[...]
    add_chunk(acc, stage, slots_ref, slot_first, arrays)
    spread[...] = acc[...].astype(BF)
    acc[...] = jnp.zeros_like(acc)
    load.wait()

    def multiply(k, carry):
        start = pl.multiple_of(k * KSTEP, KSTEP)
        acc[...] += dot_nn(adj[k], spread[pl.ds(start, KSTEP), :])
        return carry

    lax.fori_loop(0, SLOTS // KSTEP, multiply, 0)
    spread[...] = acc[...].astype(BF)
    leave(index_ref, leave_first, spread, outs)


def spread_rows(acc, arrays, slots, slot_first, adj, index, leave_first):
    feat = acc.shape[1]
    shape = arrays[0].shape
    vmem = pl.BlockSpec(memory_space=pltpu.VMEM)
    return pl.pallas_call(
        functools.partial(spread_kernel, slot_first, leave_first),
        out_shape=[jax.ShapeDtypeStruct((SLOTS, feat), BF)]
        + [jax.ShapeDtypeStruct(shape, BF)] * 4,
        in_specs=[vmem, vmem, vmem, pl.BlockSpec(memory_space=pl.ANY)] + [vmem] * 4,
        scratch_shapes=[
            pltpu.VMEM(adj.shape, BF),
            pltpu.VMEM((SLOTS, feat), F32),
            pltpu.VMEM((4 * shape[0], feat), BF),
            pltpu.SemaphoreType.DMA,
        ],
        compiler_params=params(),
        cost_estimate=cost(2 * SLOTS * feat * (SLOTS + 8 * shape[0]), 16 * 2**20),
        name="spread_rows",
    )(slots, index, acc, adj, *arrays)


def leave_kernel(first, index_ref, spread_ref, after_ref, *outs):
    leave(index_ref, first, spread_ref, outs)


def leave_rows(spread, index, first, size, after):
    feat = spread.shape[1]
    vmem = pl.BlockSpec(memory_space=pltpu.VMEM)
    return pl.pallas_call(
        functools.partial(leave_kernel, first),
        out_shape=[jax.ShapeDtypeStruct((size, feat), BF)] * 4,
        in_specs=[vmem, vmem, pl.BlockSpec(memory_space=pl.ANY)],
        compiler_params=params(),
        cost_estimate=cost(1, 1),
        name="leave_rows",
    )(index, spread, after)


def partial_sum(rows_ref, landed, row, block, masters):
    cap = rows_ref.shape[1] // 4
    rows = jnp.concatenate([a[block * cap : (block + 1) * cap, :] for a in landed], axis=0)
    return dot_nn(wide_onehot(rows_ref[row : row + 1, :], masters), rows)


def far_kernel(row, block, rows_ref, after_ref, *refs):
    total = partial_sum(rows_ref, refs[:4], row, block, 512).astype(BF)
    refs[4][...] = total[:256]
    refs[5][...] = total[256:]


def far_sums(landed, rows, row, block, after):
    feat = landed[0].shape[1]
    vmem = pl.BlockSpec(memory_space=pltpu.VMEM)
    return pl.pallas_call(
        functools.partial(far_kernel, row, block),
        out_shape=[jax.ShapeDtypeStruct((256, feat), BF)] * 2,
        in_specs=[vmem, pl.BlockSpec(memory_space=pl.ANY)] + [vmem] * 4,
        compiler_params=params(),
        cost_estimate=cost(2 * 512 * 768 * feat, 2**20),
        name="far_sums",
    )(rows, after, *landed)


def ring_kernel(halves, row, rows_ref, down_ref, up_ref, after_ref, *refs):
    landed, (down_out, up_out) = refs[:4], refs[4:]
    down = partial_sum(rows_ref, landed, row, 0, 512)
    up = partial_sum(rows_ref, landed, row + 1, 1, 512)
    if halves:
        down_out[0:256, :] = down[0:256].astype(BF)
        down_out[256:512, :] = (down[256:512] + down_ref[...].astype(F32)).astype(BF)
        up_out[0:256, :] = (up[0:256] + up_ref[...].astype(F32)).astype(BF)
        up_out[256:512, :] = up[256:512].astype(BF)
    else:
        down_out[...] = (down + down_ref[...].astype(F32)).astype(BF)
        up_out[...] = (up + up_ref[...].astype(F32)).astype(BF)


def ring_sums(landed, rows, row, down, up, after):
    feat = landed[0].shape[1]
    vmem = pl.BlockSpec(memory_space=pltpu.VMEM)
    return pl.pallas_call(
        functools.partial(ring_kernel, down.shape[0] == 256, row),
        out_shape=[jax.ShapeDtypeStruct((512, feat), BF)] * 2,
        in_specs=[vmem] * 3 + [pl.BlockSpec(memory_space=pl.ANY)] + [vmem] * 4,
        compiler_params=params(),
        cost_estimate=cost(4 * 512 * 768 * feat, 2 * 2**20),
        name="ring_sums",
    )(rows, down, up, after, *landed)


def own_kernel(masked, row, block, rows_ref, own_ref, down_ref, up_ref, *refs):
    landed, out = refs[:4], refs[-1]
    total = own_ref[...] + partial_sum(rows_ref, landed, row, block, 512)
    total = total + down_ref[...].astype(F32) + up_ref[...].astype(F32)
    if masked:
        total = jnp.where(refs[4][...].astype(F32) > 0.0, total, 0.0)
    out[...] = total.astype(BF)


def own_sums(landed, rows, row, block, own, down, up, preact):
    args = [rows, own, down, up, *landed] + ([] if preact is None else [preact])
    feat = landed[0].shape[1]
    return pl.pallas_call(
        functools.partial(own_kernel, preact is not None, row, block),
        out_shape=jax.ShapeDtypeStruct(own.shape, BF),
        compiler_params=params(),
        cost_estimate=cost(2 * 512 * 768 * feat, 2 * 2**20),
        name="own_sums",
    )(*args)


def on_device(
    features,
    preact,
    agg_first,
    agg_second,
    grad_out,
    self_first,
    neigh_first,
    self_second,
    neigh_second,
    tile_vals,
    tile_rows,
    tile_cols,
    tile_count,
    send_count,
    mirror_slot,
    master_row,
):
    groups = lax.axis_size("group")
    domains = lax.axis_size("dom")
    masters, feat = features.shape
    factor = (masters * domains * groups) ** (-0.5)
    cap = mirror_slot.shape[2]
    nx, nz = 4, domains // 4
    here = lax.axis_index("dom")
    my_z, my_x = here // nx, here % nx
    order = (-1, 1, 0, -2, 2, -3, 3, 4)
    firsts, sizes = (0, 3, 5), (3, 2, 3)

    def z_step(x, by):
        pairs = [(z * nx + c, (z + by) % nz * nx + c) for z in range(nz) for c in range(nx)]
        return lax.ppermute(x, "dom", pairs)

    def x_step(x, by):
        pairs = [(z * nx + c, z * nx + (c + by) % nx) for z in range(nz) for c in range(nx)]
        return lax.ppermute(x, "dom", pairs)

    def x_swap(parts):
        return [parts[0]] + [x_step(parts[j], j) for j in (1, 2, 3)]

    def turn(x, by, axis):
        return lax.dynamic_slice_in_dim(jnp.concatenate([x, x], axis), by, x.shape[axis], axis)

    own_lists = master_row[0].reshape(nz, nx * cap)
    z_groups = [[z * nx + c for z in range(nz)] for c in range(nx)]
    all_lists = lax.all_to_all(own_lists, "dom", 0, 0, axis_index_groups=z_groups, tiled=True)
    rows = turn(turn(all_lists.reshape(nz, nx, cap), my_z, 0), my_x, 1).astype(F32)
    live = jnp.arange(cap)[None, :] < send_count[0][:, None]
    slots = jnp.where(live, mirror_slot[0], -1).reshape(nz, nx, cap)
    slots = turn(turn(slots, my_z, 0), my_x, 1).astype(F32)

    def in_order(lists):
        return jnp.stack([lists[k % nz] for k in order])

    def back(lists):
        return jnp.stack([lists[:, -j % nx] for j in range(nx)], axis=1)

    def by_step(lists):
        parts = [
            lists[f : f + n].transpose(1, 0, 2).reshape(n, nx * cap)
            for f, n in zip(firsts, sizes)
        ]
        return jnp.concatenate(parts, axis=0)

    rows, slots = in_order(rows), in_order(slots)
    pick_lists = rows.reshape(-1, EDGE)
    sum_lists = back(rows).reshape(nz, nx * cap)
    put_lists = by_step(back(slots))
    leave_lists = by_step(slots).reshape(-1, EDGE)
    per = nx * cap // EDGE

    def mirror_push(pushed, after):
        half = masters // 2
        down1, up1 = z_step(pushed, 1), z_step(pushed, -1)
        near = pick_rows([(down1,), (up1,), (pushed,)], pick_lists, 0, after)
        arrived = [x_swap(near)]
        down2, up2 = tie((z_step(down1, 1), z_step(up1, -1)), near[0])
        middle = pick_rows([(down2,), (up2,)], pick_lists, 3, near[:1])
        arrived.append(x_swap(middle))
        down3, up3 = tie((z_step(down2, 1), z_step(up2, -1)), middle[0])
        far = (z_step(down3[:half], 1), z_step(up3[half:], -1))
        acc = early_slots(arrived[0], None, put_lists, firsts[0], middle[0])
        last = pick_rows([(down3,), (up3,), far], pick_lists, 5, [acc, *arrived[1][1:]])
        arrived.append(x_swap(last))
        acc = early_slots(arrived[1], acc, put_lists, firsts[1], last[0])
        return arrived, acc

    def mirror_return(arrived, acc, adj):
        spread, *parts = spread_rows(
            acc, arrived[2], put_lists, firsts[2], adj, leave_lists, firsts[2] * per
        )
        landed = [None, None, x_swap(parts)]
        after = parts[0]
        for c in (1, 0):
            parts = leave_rows(spread, leave_lists, firsts[c] * per, sizes[c] * cap, after)
            landed[c] = x_swap(parts)
            after = parts[0]
        up, down = far_sums(landed[2], sum_lists, 7, 2, after)
        up, down = z_step(up, 1), z_step(down, -1)
        for c in (2, 1, 0):
            soon = landed[max(c - 1, 0)][2]
            down, up = ring_sums(landed[c], sum_lists, firsts[c], down, up, soon)
            up, down = z_step(up, 1), z_step(down, -1)
        return landed[0], down, up

    def push(upstream, w_neigh, after):
        pushed = jnp.einsum("nf,gf->ng", upstream, w_neigh, preferred_element_type=F32).astype(BF)
        return mirror_push(pushed, after)

    def finish(upstream, w_self, arrived, acc, adj, mask):
        own = jnp.einsum("nf,gf->ng", upstream, w_self, preferred_element_type=F32)
        landed, down, up = mirror_return(arrived, acc, adj)
        return own_sums(landed, sum_lists, 2, 2, own, down, up, mask)

    def swap(x, axis="dom"):
        return lax.all_to_all(x, axis, split_axis=0, concat_axis=0, tiled=True)

    def grads(inputs, stored, upstream):
        both = [
            jnp.einsum("nf,ng->fg", part, upstream, preferred_element_type=F32)
            for part in (inputs, stored)
        ]
        return jnp.concatenate(both, axis=0) * factor

    def scatter_sum(total):
        height = total.shape[0] // groups
        part = swap(total.reshape(groups, height, feat), "group")
        part = jnp.sum(part.astype(F32), axis=0)
        return jnp.sum(swap(part.reshape(domains, height // domains, feat)), axis=0)

    activated = jnp.maximum(preact, 0.0)
    weights_two = grads(activated, agg_second, grad_out)
    arrived, acc = push(grad_out, neigh_second, [])
    adj = dense_adjacency(tile_vals, tile_rows[0], tile_cols[0], tile_count, acc)
    upstream = finish(grad_out, self_second, arrived, acc, adj, preact)

    weights_one = grads(features, agg_first, upstream)
    both = jnp.concatenate([weights_one, weights_two], axis=0).astype(BF)
    piece = scatter_sum(both)
    arrived, acc = push(upstream, neigh_first, [both])
    input_grad = finish(upstream, self_first, arrived, acc, adj, None)
    weights = lax.all_gather(piece, ("group", "dom"), axis=0, tiled=True)
    return (input_grad, weights.reshape(4, feat, feat))


def solution(mesh):
    every = ("group", "dom")
    in_specs = (
        (P(every, None),) * 5
        + (P(),) * 4
        + (P(every, None, None), P(every, None), P(every, None), P(every), P(every, None))
        + (P(every, None, None),) * 2
    )
    out_specs = (P(every, None), P())
    return jax.shard_map(
        on_device, mesh=mesh, in_specs=in_specs, out_specs=out_specs, check_vma=False
    )
```

```python
import functools

import jax
import jax.numpy as jnp
from jax import lax
from jax.experimental import pallas as pl
from jax.experimental.pallas import tpu as pltpu
from jax.sharding import PartitionSpec as P

SLOTS = 2048
EDGE = 128
KSTEP = 512
BF = jnp.bfloat16
F32 = jnp.float32
BIG = 56 * 1024 * 1024


def params():
    return pltpu.CompilerParams(vmem_limit_bytes=BIG)


def dot_nt(a, b):
    return lax.dot_general(a, b, (((1,), (1,)), ((), ())), preferred_element_type=F32)


def dot_nn(a, b):
    return lax.dot_general(a, b, (((1,), (0,)), ((), ())), preferred_element_type=F32)


def wide_onehot(index_row, height):
    high = jnp.floor(index_row * (1.0 / EDGE))
    low = index_row - high * EDGE
    iota = lax.broadcasted_iota(jnp.int32, (EDGE, index_row.shape[1]), 0).astype(F32)
    base = jnp.where(iota == low, 1.0, 0.0).astype(BF)
    parts = [
        base * jnp.where(high == float(b), 1.0, 0.0).astype(BF) for b in range(height // EDGE)
    ]
    return jnp.concatenate(parts, axis=0)


def tall_onehot(index_row, width):
    column = jnp.transpose(jnp.broadcast_to(index_row, (EDGE, EDGE)))
    high = jnp.floor(column * (1.0 / EDGE))
    low = column - high * EDGE
    iota = lax.broadcasted_iota(jnp.int32, (EDGE, EDGE), 1).astype(F32)
    base = jnp.where(iota == low, 1.0, 0.0).astype(BF)
    high = high.astype(BF)
    none = jnp.zeros_like(base)
    parts = [jnp.where(high == jnp.full_like(high, b), base, none) for b in range(width // EDGE)]
    return jnp.concatenate(parts, axis=1)


def dense_kernel(rows_ref, cols_ref, count_ref, vals_ref, after_ref, out_ref, acc):
    step = pl.program_id(0)
    per = vals_ref.shape[0]

    @pl.when(step == 0)
    def _():
        def clear(i, carry):
            acc[i] = jnp.zeros((EDGE, EDGE), F32)
            return carry

        lax.fori_loop(0, acc.shape[0], clear, 0)

    first = step * per
    live = jnp.clip(count_ref[0] - first, 0, per)

    def add(i, carry):
        at = rows_ref[first + i] * 16 + cols_ref[first + i]
        acc[at] += vals_ref[i].astype(F32)
        return carry

    lax.fori_loop(0, live, add, 0)

    @pl.when(step == pl.num_programs(0) - 1)
    def _():
        def flip(j, carry):
            start = pl.multiple_of(j * EDGE, EDGE)
            for i in range(16):
                block = jnp.transpose(acc[i * 16 + j].astype(BF))
                lane = (i % 4) * EDGE
                out_ref[i // 4, pl.ds(start, EDGE), lane : lane + EDGE] = block
            return carry

        lax.fori_loop(0, 16, flip, 0)


def dense_adjacency(tile_vals, rows, cols, count, after):
    tiles = tile_vals.shape[0]
    per = 32
    return pl.pallas_call(
        dense_kernel,
        out_shape=jax.ShapeDtypeStruct((SLOTS // KSTEP, SLOTS, KSTEP), BF),
        grid_spec=pltpu.PrefetchScalarGridSpec(
            num_scalar_prefetch=3,
            grid=(tiles // per,),
            in_specs=[
                pl.BlockSpec((per, EDGE, EDGE), lambda i, *_: (i, 0, 0)),
                pl.BlockSpec(memory_space=pl.ANY),
            ],
            out_specs=pl.BlockSpec((SLOTS // KSTEP, SLOTS, KSTEP), lambda i, *_: (0, 0, 0)),
            scratch_shapes=[pltpu.VMEM((256, EDGE, EDGE), F32)],
        ),
        compiler_params=params(),
        cost_estimate=cost(1, 1),
        name="dense_adjacency",
    )(rows, cols, count, tile_vals, after)


def cost(flops, size):
    return pl.CostEstimate(flops=flops, bytes_accessed=size, transcendentals=0)


def tall_rows(index_ref, first, count, width):
    return jnp.concatenate(
        [tall_onehot(index_ref[first + j : first + j + 1, :], width) for j in range(count)], axis=0
    )


def split_rows(value, outs):
    size = outs[0].shape[0]
    for j, out in enumerate(outs):
        out[...] = value[j * size : (j + 1) * size, :]


def tie_kernel(*refs):
    pass


def tie(arrays, after):
    anywhere = pl.BlockSpec(memory_space=pl.ANY)
    return pl.pallas_call(
        tie_kernel,
        out_shape=[jax.ShapeDtypeStruct(a.shape, a.dtype) for a in arrays],
        in_specs=[anywhere] * (len(arrays) + 1),
        out_specs=[anywhere] * len(arrays),
        input_output_aliases={i: i for i in range(len(arrays))},
        cost_estimate=cost(1, 1),
        name="tie",
    )(*arrays, after)


def pick_kernel(first, parts, waits, index_ref, *refs):
    refs = refs[waits:]
    sources, outs = refs[: sum(parts)], refs[sum(parts) :]
    cap = outs[0].shape[0] // len(parts)
    per = 4 * cap // EDGE
    at = 0
    for b, pieces in enumerate(parts):
        block = jnp.concatenate([r[...] for r in sources[at : at + pieces]], axis=0)
        at += pieces
        hot = tall_rows(index_ref, (first + b) * per, per, block.shape[0])
        rows = dot_nn(hot, block).astype(BF)
        for j in range(4):
            outs[j][b * cap : (b + 1) * cap, :] = rows[j * cap : (j + 1) * cap, :]


def pick_rows(blocks, index, first, after):
    feat = blocks[0][0].shape[1]
    n = len(blocks)
    cap = index.size // 32
    vmem = pl.BlockSpec(memory_space=pltpu.VMEM)
    return pl.pallas_call(
        functools.partial(pick_kernel, first, tuple(len(b) for b in blocks), len(after)),
        out_shape=[jax.ShapeDtypeStruct((n * cap, feat), BF)] * 4,
        in_specs=[vmem]
        + [pl.BlockSpec(memory_space=pl.ANY)] * len(after)
        + [vmem] * sum(len(b) for b in blocks),
        compiler_params=params(),
        cost_estimate=cost(8 * n * cap * 512 * feat, n * 2**20),
        name="pick_rows",
    )(index, *after, *[piece for b in blocks for piece in b])


def add_chunk(acc, stage, slots_ref, first, arrays):
    size = arrays[0].shape[0]
    for j, a in enumerate(arrays):
        stage[j * size : (j + 1) * size, :] = a[...]
    width = slots_ref.shape[1]
    for p in range(4 * size // width):
        hot = wide_onehot(slots_ref[first + p : first + p + 1, :], SLOTS)
        acc[...] += dot_nn(hot, stage[p * width : (p + 1) * width, :])


def early_kernel(first, slots_ref, after_ref, *refs):
    out, stage = refs[-2:]
    if len(refs) == 7:
        out[...] = refs[4][...]
    else:
        out[...] = jnp.zeros_like(out)
    add_chunk(out, stage, slots_ref, first, refs[:4])


def early_slots(arrays, acc, slots, first, after):
    size, feat = arrays[0].shape
    vmem = pl.BlockSpec(memory_space=pltpu.VMEM)
    args = [*arrays] + ([] if acc is None else [acc])
    return pl.pallas_call(
        functools.partial(early_kernel, first),
        out_shape=jax.ShapeDtypeStruct((SLOTS, feat), F32),
        in_specs=[vmem, pl.BlockSpec(memory_space=pl.ANY)] + [vmem] * len(args),
        scratch_shapes=[pltpu.VMEM((4 * size, feat), BF)],
        compiler_params=params(),
        cost_estimate=cost(1, 1),
        name="early_slots",
    )(slots, after, *args)


def leave(index_ref, first, spread_ref, outs):
    size = outs[0].shape[0]
    per = 2 * size // EDGE
    for h in range(2):
        hot = tall_rows(index_ref, first + h * per, per, SLOTS)
        rows = dot_nn(hot, spread_ref[...]).astype(BF)
        outs[2 * h][...] = rows[:size, :]
        outs[2 * h + 1][...] = rows[size:, :]


def spread_kernel(slot_first, leave_first, slots_ref, index_ref, acc_in, adj_hbm, *refs):
    arrays, spread, outs = refs[:4], refs[4], refs[5:9]
    adj, acc, stage, sem = refs[9:]
    load = pltpu.make_async_copy(adj_hbm, adj, sem)
    load.start()
    acc[...] = acc_in[...]
    add_chunk(acc, stage, slots_ref, slot_first, arrays)
    spread[...] = acc[...].astype(BF)
    acc[...] = jnp.zeros_like(acc)
    load.wait()

    def multiply(k, carry):
        start = pl.multiple_of(k * KSTEP, KSTEP)
        acc[...] += dot_nn(adj[k], spread[pl.ds(start, KSTEP), :])
        return carry

    lax.fori_loop(0, SLOTS // KSTEP, multiply, 0)
    spread[...] = acc[...].astype(BF)
    leave(index_ref, leave_first, spread, outs)


def spread_rows(acc, arrays, slots, slot_first, adj, index, leave_first):
    feat = acc.shape[1]
    shape = arrays[0].shape
    vmem = pl.BlockSpec(memory_space=pltpu.VMEM)
    return pl.pallas_call(
        functools.partial(spread_kernel, slot_first, leave_first),
        out_shape=[jax.ShapeDtypeStruct((SLOTS, feat), BF)]
        + [jax.ShapeDtypeStruct(shape, BF)] * 4,
        in_specs=[vmem, vmem, vmem, pl.BlockSpec(memory_space=pl.ANY)] + [vmem] * 4,
        scratch_shapes=[
            pltpu.VMEM(adj.shape, BF),
            pltpu.VMEM((SLOTS, feat), F32),
            pltpu.VMEM((4 * shape[0], feat), BF),
            pltpu.SemaphoreType.DMA,
        ],
        compiler_params=params(),
        cost_estimate=cost(2 * SLOTS * feat * (SLOTS + 8 * shape[0]), 16 * 2**20),
        name="spread_rows",
    )(slots, index, acc, adj, *arrays)


def leave_kernel(first, index_ref, spread_ref, after_ref, *outs):
    leave(index_ref, first, spread_ref, outs)


def leave_rows(spread, index, first, size, after):
    feat = spread.shape[1]
    vmem = pl.BlockSpec(memory_space=pltpu.VMEM)
    return pl.pallas_call(
        functools.partial(leave_kernel, first),
        out_shape=[jax.ShapeDtypeStruct((size, feat), BF)] * 4,
        in_specs=[vmem, vmem, pl.BlockSpec(memory_space=pl.ANY)],
        compiler_params=params(),
        cost_estimate=cost(1, 1),
        name="leave_rows",
    )(index, spread, after)


def partial_sum(rows_ref, landed, row, block, masters):
    cap = rows_ref.shape[1] // 4
    rows = jnp.concatenate([a[block * cap : (block + 1) * cap, :] for a in landed], axis=0)
    return dot_nn(wide_onehot(rows_ref[row : row + 1, :], masters), rows)


def far_kernel(row, block, rows_ref, after_ref, *refs):
    total = partial_sum(rows_ref, refs[:4], row, block, 512).astype(BF)
    refs[4][...] = total[:256]
    refs[5][...] = total[256:]


def far_sums(landed, rows, row, block, after):
    feat = landed[0].shape[1]
    vmem = pl.BlockSpec(memory_space=pltpu.VMEM)
    return pl.pallas_call(
        functools.partial(far_kernel, row, block),
        out_shape=[jax.ShapeDtypeStruct((256, feat), BF)] * 2,
        in_specs=[vmem, pl.BlockSpec(memory_space=pl.ANY)] + [vmem] * 4,
        compiler_params=params(),
        cost_estimate=cost(2 * 512 * 768 * feat, 2**20),
        name="far_sums",
    )(rows, after, *landed)


def ring_kernel(halves, row, rows_ref, down_ref, up_ref, after_ref, *refs):
    landed, (down_out, up_out) = refs[:4], refs[4:]
    down = partial_sum(rows_ref, landed, row, 0, 512)
    up = partial_sum(rows_ref, landed, row + 1, 1, 512)
    if halves:
        down_out[0:256, :] = down[0:256].astype(BF)
        down_out[256:512, :] = (down[256:512] + down_ref[...].astype(F32)).astype(BF)
        up_out[0:256, :] = (up[0:256] + up_ref[...].astype(F32)).astype(BF)
        up_out[256:512, :] = up[256:512].astype(BF)
    else:
        down_out[...] = (down + down_ref[...].astype(F32)).astype(BF)
        up_out[...] = (up + up_ref[...].astype(F32)).astype(BF)


def ring_sums(landed, rows, row, down, up, after):
    feat = landed[0].shape[1]
    vmem = pl.BlockSpec(memory_space=pltpu.VMEM)
    return pl.pallas_call(
        functools.partial(ring_kernel, down.shape[0] == 256, row),
        out_shape=[jax.ShapeDtypeStruct((512, feat), BF)] * 2,
        in_specs=[vmem] * 3 + [pl.BlockSpec(memory_space=pl.ANY)] + [vmem] * 4,
        compiler_params=params(),
        cost_estimate=cost(4 * 512 * 768 * feat, 2 * 2**20),
        name="ring_sums",
    )(rows, down, up, after, *landed)


def own_kernel(masked, row, block, rows_ref, own_ref, down_ref, up_ref, *refs):
    landed, out = refs[:4], refs[-1]
    total = own_ref[...] + partial_sum(rows_ref, landed, row, block, 512)
    total = total + down_ref[...].astype(F32) + up_ref[...].astype(F32)
    if masked:
        total = jnp.where(refs[4][...].astype(F32) > 0.0, total, 0.0)
    out[...] = total.astype(BF)


def own_sums(landed, rows, row, block, own, down, up, preact):
    args = [rows, own, down, up, *landed] + ([] if preact is None else [preact])
    feat = landed[0].shape[1]
    return pl.pallas_call(
        functools.partial(own_kernel, preact is not None, row, block),
        out_shape=jax.ShapeDtypeStruct(own.shape, BF),
        compiler_params=params(),
        cost_estimate=cost(2 * 512 * 768 * feat, 2 * 2**20),
        name="own_sums",
    )(*args)


def on_device(
    features,
    preact,
    agg_first,
    agg_second,
    grad_out,
    self_first,
    neigh_first,
    self_second,
    neigh_second,
    tile_vals,
    tile_rows,
    tile_cols,
    tile_count,
    send_count,
    mirror_slot,
    master_row,
):
    groups = lax.axis_size("group")
    domains = lax.axis_size("dom")
    masters, feat = features.shape
    factor = (masters * domains * groups) ** (-0.5)
    cap = mirror_slot.shape[2]
    nx, nz = 4, domains // 4
    here = lax.axis_index("dom")
    my_z, my_x = here // nx, here % nx
    order = (-1, 1, 0, -2, 2, -3, 3, 4)
    firsts, sizes = (0, 3, 5), (3, 2, 3)

    def z_step(x, by):
        pairs = [(z * nx + c, (z + by) % nz * nx + c) for z in range(nz) for c in range(nx)]
        return lax.ppermute(x, "dom", pairs)

    def x_step(x, by):
        pairs = [(z * nx + c, z * nx + (c + by) % nx) for z in range(nz) for c in range(nx)]
        return lax.ppermute(x, "dom", pairs)

    def x_swap(parts):
        return [parts[0]] + [x_step(parts[j], j) for j in (1, 2, 3)]

    def turn(x, by, axis):
        return lax.dynamic_slice_in_dim(jnp.concatenate([x, x], axis), by, x.shape[axis], axis)

    own_lists = master_row[0].reshape(nz, nx * cap)
    z_groups = [[z * nx + c for z in range(nz)] for c in range(nx)]
    all_lists = lax.all_to_all(own_lists, "dom", 0, 0, axis_index_groups=z_groups, tiled=True)
    rows = turn(turn(all_lists.reshape(nz, nx, cap), my_z, 0), my_x, 1).astype(F32)
    live = jnp.arange(cap)[None, :] < send_count[0][:, None]
    slots = jnp.where(live, mirror_slot[0], -1).reshape(nz, nx, cap)
    slots = turn(turn(slots, my_z, 0), my_x, 1).astype(F32)

    def in_order(lists):
        return jnp.stack([lists[k % nz] for k in order])

    def back(lists):
        return jnp.stack([lists[:, -j % nx] for j in range(nx)], axis=1)

    def by_step(lists):
        parts = [
            lists[f : f + n].transpose(1, 0, 2).reshape(n, nx * cap)
            for f, n in zip(firsts, sizes)
        ]
        return jnp.concatenate(parts, axis=0)

    rows, slots = in_order(rows), in_order(slots)
    pick_lists = rows.reshape(-1, EDGE)
    sum_lists = back(rows).reshape(nz, nx * cap)
    put_lists = by_step(back(slots))
    leave_lists = by_step(slots).reshape(-1, EDGE)
    per = nx * cap // EDGE

    def mirror_push(pushed, waits):
        half = masters // 2
        down1, up1 = z_step(pushed, 1), z_step(pushed, -1)
        near = pick_rows([(down1,), (up1,), (pushed,)], pick_lists, 0, [])
        arrived = [x_swap(near)]
        down2, up2 = tie((z_step(down1, 1), z_step(up1, -1)), near[0])
        middle = pick_rows([(down2,), (up2,)], pick_lists, 3, [near[0]] + waits[0])
        arrived.append(x_swap(middle))
        down3, up3 = tie((z_step(down2, 1), z_step(up2, -1)), middle[0])
        far = (z_step(down3[:half], 1), z_step(up3[half:], -1))
        acc = early_slots(arrived[0], None, put_lists, firsts[0], middle[0])
        last = pick_rows([(down3,), (up3,), far], pick_lists, 5, [acc, *arrived[1][1:]] + waits[1])
        arrived.append(x_swap(last))
        acc = early_slots(arrived[1], acc, put_lists, firsts[1], last[0])
        return arrived, acc

    def mirror_return(arrived, acc, adj):
        spread, *parts = spread_rows(
            acc, arrived[2], put_lists, firsts[2], adj, leave_lists, firsts[2] * per
        )
        landed = [None, None, x_swap(parts)]
        after = parts[0]
        for c in (1, 0):
            parts = leave_rows(spread, leave_lists, firsts[c] * per, sizes[c] * cap, after)
            landed[c] = x_swap(parts)
            after = parts[0]
        up, down = far_sums(landed[2], sum_lists, 7, 2, after)
        up, down = z_step(up, 1), z_step(down, -1)
        for c in (2, 1, 0):
            soon = landed[1 if c else 0][2]
            down, up = ring_sums(landed[c], sum_lists, firsts[c], down, up, soon)
            up, down = z_step(up, 1), z_step(down, -1)
        return landed[0], down, up

    def push(upstream, w_neigh, waits):
        pushed = jnp.einsum("nf,gf->ng", upstream, w_neigh, preferred_element_type=F32).astype(BF)
        return mirror_push(pushed, waits)

    def finish(upstream, w_self, arrived, acc, adj, mask):
        own = jnp.einsum("nf,gf->ng", upstream, w_self, preferred_element_type=F32)
        landed, down, up = mirror_return(arrived, acc, adj)
        return own_sums(landed, sum_lists, 2, 2, own, down, up, mask)

    def swap(x, axis="dom"):
        return lax.all_to_all(x, axis, split_axis=0, concat_axis=0, tiled=True)

    def grads(inputs, stored, upstream):
        both = [
            jnp.einsum("nf,ng->fg", part, upstream, preferred_element_type=F32)
            for part in (inputs, stored)
        ]
        return jnp.concatenate(both, axis=0) * factor

    def group_sum(total):
        parts = swap(total.reshape(groups, -1, feat), "group")
        return jnp.sum(parts.astype(F32), axis=0)

    def domain_sum(part):
        return jnp.sum(swap(part.reshape(domains, -1, feat)), axis=0)

    activated = jnp.maximum(preact, 0.0)
    weights_two = grads(activated, agg_second, grad_out)
    arrived, acc = push(grad_out, neigh_second, ([], []))
    adj = dense_adjacency(tile_vals, tile_rows[0], tile_cols[0], tile_count, acc)
    upstream = finish(grad_out, self_second, arrived, acc, adj, preact)

    weights_one = grads(features, agg_first, upstream)
    both = jnp.concatenate([weights_one, weights_two], axis=0).astype(BF)
    part = group_sum(both)
    piece = domain_sum(part)
    arrived, acc = push(upstream, neigh_first, ([both], [piece]))
    input_grad = finish(upstream, self_first, arrived, acc, adj, None)
    weights = lax.all_gather(piece, ("group", "dom"), axis=0, tiled=True)
    return (input_grad, weights.reshape(4, feat, feat))


def solution(mesh):
    every = ("group", "dom")
    in_specs = (
        (P(every, None),) * 5
        + (P(),) * 4
        + (P(every, None, None), P(every, None), P(every, None), P(every), P(every, None))
        + (P(every, None, None),) * 2
    )
    out_specs = (P(every, None), P())
    return jax.shard_map(
        on_device, mesh=mesh, in_specs=in_specs, out_specs=out_specs, check_vma=False
    )
```
